32 devices in a mesh: groups: 2 (over x), dp: 2 (over core), tensor: 8 (over z, y).
Axes of the slice: x: 2, y: 2, z: 4, core: 2. Of those that a mesh axis runs over, the one named last changes fastest.
Arguments:
- hidden: bfloat16 [1536, 16384], P(('groups', 'dp'), 'tensor'), parts along dimension 0, may hold values from -6 to 6
- down_matrix: bfloat16 [16384, 8192], P('tensor'), may hold values from -0.0625 to 0.0625
- rank_input_map: bfloat16 [32, 16, 16384], P(None, None, 'tensor'), may hold values from -0.046875 to 0.046875
- rank_output_map: bfloat16 [32, 16, 8192], P(None, None, 'tensor'), may hold values from -0.75 to 0.75
- job_row_counts: int32 [64], P('groups'), parts along dimension 0, may hold values from 1 to 192, 768 in all
- output_gradient: bfloat16 [1536, 8192], P(('groups', 'dp'), 'tensor'), parts along dimension 0, may hold values from -6 to 6
Outputs:
- mixed: bfloat16 [1536, 8192], P(('groups', 'dp'), 'tensor'), parts along dimension 0
- grad_hidden: bfloat16 [1536, 16384], P(('groups', 'dp'), 'tensor'), parts along dimension 0
- grad_a: float32 [64, 16, 16384], P(('groups', 'dp'), None, 'tensor'), parts along dimension 0
- grad_b: float32 [64, 16, 8192], P(('groups', 'dp'), None, 'tensor'), parts along dimension 0
The draws below stay inside these ranges and needn't reach their ends.
There are 2 independent parts, one for each index of `groups`. The reference program is written for one: setup_inputs(seed, part) draws one part's arguments, and reference() takes and returns one part's arrays. A program takes and returns all parts, laid end to end along the dimension named above; an argument that names none is the same for every part. Nothing has to cross between parts.
Inputs may be any that keep to these rules, and one draw needn't show every extreme that they name: `job_row_counts`: the counts sum to 768 and the largest is exactly 192.
All inputs are finite; a program needn't handle non-finite values.
Results may differ from the reference program's by a relative error of at most 0.014.
Values may be sent and summed in bfloat16 or wider, within the bound.
A program may use at most 192 MiB of HBM per device.

```python
import math
import jax
import jax.numpy as jnp
import numpy as np
from jax import lax

MODEL_WIDTH = 8192
HIDDEN_UNITS = 16384
ADAPTER_RANK = 16
PACKED_JOBS = 32
TOKENS = 768
N_TENSOR = 8


def strengthened(drawn, stream_key, source, target, parts, factor):
    owner, partner = [(jnp.arange(drawn.shape[axis_at]) // (drawn.shape[axis_at] // parts)).reshape([-1 if axis == axis_at else 1 for axis in range(drawn.ndim)]) for axis_at in (source, target)]
    chosen = jax.random.permutation(stream_key, parts)[partner]
    strong = (owner == chosen) | (owner == (partner + parts // 2) % parts)
    return jnp.where(strong, factor * drawn, drawn)


def steps_of(key, extent, shards, smallest, largest):
    loudness = 1.0
    for position, blocks in shards:
        heights = jax.random.uniform(jax.random.fold_in(jax.random.fold_in(key, 6), position), (blocks,), jnp.float32, smallest / len(shards), largest / len(shards))
        loudness = loudness * jnp.repeat(jnp.exp(heights), extent[position] // blocks).reshape((-1,) + (1,) * (len(extent) - 1 - position))
    return loudness


def split_up(number_of, total, most, slope):
    loads = [(1 << 20) // math.isqrt(grade ** slope) + 1 for grade in range(2, number_of + 1)]
    spare, holding = total - most - (number_of - 1), [1] * (number_of - 1)
    while spare > 0:
        movable = [i for i in range(number_of - 1) if holding[i] < most]
        mass, budget = sum([loads[i] for i in movable]), spare
        for i in movable:
            extra = min(most - holding[i], max(1, budget * loads[i] // mass), spare)
            holding[i] = holding[i] + extra
            spare = spare - extra
    return np.array([most] + holding)


def ragged(own_key, count, total, limit, slope):
    if count == 2:
        one = jax.random.randint(own_key, (), max(1, total - limit), min(limit, total - 1) + 1)
        return jnp.stack([one, total - one])
    sizes = jnp.asarray(split_up(count, total, limit, slope), jnp.int32)
    twos = (count - 1) // 2
    donor, sink = sizes[1:1 + 2 * twos:2], sizes[2:2 + 2 * twos:2]
    slack = jnp.minimum(donor - 1, limit - sink)
    passed = jax.random.randint(jax.random.fold_in(own_key, 1), (twos,), 0, 1 << 20) % (slack + 1)
    sizes = sizes.at[1:1 + 2 * twos:2].set(donor - passed).at[2:2 + 2 * twos:2].set(sink + passed)
    return sizes[jax.random.permutation(jax.random.fold_in(own_key, 2), count)]


def scatter_about(key, extent, scale, reach, pieces=(), held_as=jnp.bfloat16):
    drawn = jax.random.normal(key, extent, jnp.float32) * scale
    if len(pieces) > 0:
        drawn = steps_of(key, extent, pieces, -0.22, 0.18) * drawn
    return jnp.clip(drawn, min=-reach, max=reach).astype(held_as)


def bell_draw_with(key, shape, scale, most, pieces, heavy, held_as=jnp.bfloat16):
    array = scale * jax.random.normal(key, shape, jnp.float32)
    if pieces:
        array = array * steps_of(key, shape, pieces, -0.22, 0.18)
    return jnp.clip(strengthened(array, jax.random.fold_in(key, 3), *heavy), -most, most).astype(held_as)


def setup_inputs(seed: int = 0, part: int = 0) -> dict:
    key_of = jax.random.split(jax.random.key(seed), 7)
    part_keys = jax.random.split(jax.random.fold_in(key_of[6], part), 7)
    hidden = scatter_about(part_keys[0], (TOKENS, HIDDEN_UNITS), 1.0, 6.0, ((0, 2), (1, 8)))
    down_matrix = bell_draw_with(key_of[1], (HIDDEN_UNITS, MODEL_WIDTH), HIDDEN_UNITS ** -0.5, 0.0625, ((0, 8),), (0, 1, 8, 2.0))
    rank_input_map = scatter_about(key_of[2], (PACKED_JOBS, ADAPTER_RANK, HIDDEN_UNITS), HIDDEN_UNITS ** -0.5, 0.046875, ((2, 8),))
    rank_output_map = scatter_about(key_of[3], (PACKED_JOBS, ADAPTER_RANK, MODEL_WIDTH), (4 * ADAPTER_RANK) ** -0.5, 0.75, ((2, 8),))
    job_row_counts = ragged(part_keys[4], PACKED_JOBS, TOKENS, TOKENS // 4, 2).astype(jnp.int32)
    output_gradient = scatter_about(part_keys[5], (TOKENS, MODEL_WIDTH), 1.0, 6.0, ((0, 2), (1, 8)))
    return {"hidden": hidden, "down_matrix": down_matrix, "rank_input_map": rank_input_map, "rank_output_map": rank_output_map, "job_row_counts": job_row_counts, "output_gradient": output_gradient}


SCALE = 2.0


def membership(job_row_counts, rows):
    ends = jnp.cumsum(job_row_counts)
    starts = ends - job_row_counts
    positions = lax.iota(jnp.int32, rows)
    inside = (positions[None, :] >= starts[:, None]) & (positions[None, :] < ends[:, None])
    return inside.astype(jnp.float32)


def select(spread, member, rank_count):
    job_count = member.shape[0]
    return jnp.sum(spread.reshape(job_count, rank_count, member.shape[1]) * member[:, None, :], axis=0)


def expand(values, member):
    job_count, rows = member.shape
    full = member[:, None, :] * values.astype(jnp.float32)[None, :, :]
    return full.reshape(job_count * values.shape[0], rows).astype(jnp.bfloat16)


def reference(hidden, down_matrix, rank_input_map, rank_output_map, job_row_counts, output_gradient):
    member = membership(job_row_counts, TOKENS)
    input_adapter = rank_input_map.reshape(PACKED_JOBS * ADAPTER_RANK, HIDDEN_UNITS)
    output_adapter = rank_output_map.reshape(PACKED_JOBS * ADAPTER_RANK, MODEL_WIDTH)
    dims = (((1,), (1,)), ((), ()))
    low = select(lax.dot_general(input_adapter, hidden, dims, preferred_element_type=jnp.float32), member, ADAPTER_RANK)
    low_scaled = (SCALE * low).astype(jnp.bfloat16)
    low_wide = expand(low_scaled, member)
    block = HIDDEN_UNITS // N_TENSOR
    base = jnp.zeros((TOKENS, MODEL_WIDTH), jnp.float32)
    for index in range(N_TENSOR):
        part = jnp.dot(hidden[:, index * block:(index + 1) * block], down_matrix[index * block:(index + 1) * block], preferred_element_type=jnp.float32)
        rounded = lax.optimization_barrier(part.astype(jnp.bfloat16))
        base = base + rounded.astype(jnp.float32)
    lead = (((0,), (0,)), ((), ()))
    adapter_out = lax.dot_general(low_wide, output_adapter, lead, preferred_element_type=jnp.float32)
    mixed = (base + adapter_out).astype(jnp.bfloat16)
    back_low = select(lax.dot_general(output_adapter, output_gradient, dims, preferred_element_type=jnp.float32), member, ADAPTER_RANK)
    back_scaled = (SCALE * back_low).astype(jnp.bfloat16)
    back_wide = expand(back_scaled, member)
    grad_b = jnp.dot(low_wide, output_gradient, preferred_element_type=jnp.float32).reshape(PACKED_JOBS, ADAPTER_RANK, MODEL_WIDTH)
    grad_a = jnp.dot(back_wide, hidden, preferred_element_type=jnp.float32).reshape(PACKED_JOBS, ADAPTER_RANK, HIDDEN_UNITS)
    through = lax.dot_general(output_gradient, down_matrix, dims, preferred_element_type=jnp.float32)
    adapter_back = lax.dot_general(back_wide, input_adapter, lead, preferred_element_type=jnp.float32)
    grad_hidden = (through + adapter_back).astype(jnp.bfloat16)
    return mixed, grad_hidden, grad_a, grad_b
```

```python
import jax
import jax.numpy as jnp
from jax import lax
from jax.experimental import pallas as pl
from jax.experimental.pallas import tpu as pltpu
from jax.sharding import PartitionSpec as P

SCALE = 2.0


def select(spread, member, rank_count):
    job_count = member.shape[0]
    return jnp.sum(
        spread.reshape(job_count, rank_count, member.shape[1]) * member[:, None, :], axis=0
    )


def expand(values, member):
    job_count, rows = member.shape
    full = member[:, None, :] * values.astype(jnp.float32)[None, :, :]
    return full.reshape(job_count * values.shape[0], rows).astype(jnp.bfloat16)


def body(hidden, down_matrix, rank_input_map, rank_output_map, job_row_counts, output_gradient):
    rows_dev, local_hidden = hidden.shape
    job_count, rank_count, local_width = rank_output_map.shape
    input_adapter = rank_input_map.reshape(job_count * rank_count, local_hidden)
    output_adapter = rank_output_map.reshape(job_count * rank_count, local_width)
    positions = lax.axis_index("dp") * rows_dev + lax.iota(jnp.int32, rows_dev)
    ends = jnp.cumsum(job_row_counts)
    starts = ends - job_row_counts
    member = (
        (positions[None, :] >= starts[:, None]) & (positions[None, :] < ends[:, None])
    ).astype(jnp.float32)
    dims = (((1,), (1,)), ((), ()))
    lead = (((0,), (0,)), ((), ()))
    low_part = select(
        lax.dot_general(input_adapter, hidden, dims, preferred_element_type=jnp.float32),
        member,
        rank_count,
    )
    back_part = select(
        lax.dot_general(output_adapter, output_gradient, dims, preferred_element_type=jnp.float32),
        member,
        rank_count,
    )
    low = lax.psum(low_part, "tensor")
    back_low = lax.psum(back_part, "tensor")
    low_wide = expand((SCALE * low).astype(jnp.bfloat16), member)
    back_wide = expand((SCALE * back_low).astype(jnp.bfloat16), member)
    cross = (((0,), (1,)), ((), ()))
    weight_cols = down_matrix
    base = (
        lax.psum_scatter(
            lax.dot_general(weight_cols, hidden, cross, preferred_element_type=jnp.float32).astype(
                jnp.bfloat16
            ),
            "tensor",
            scatter_dimension=0,
            tiled=True,
        )
        .astype(jnp.float32)
        .T
    )
    adapter_out = lax.dot_general(
        low_wide, output_adapter, lead, preferred_element_type=jnp.float32
    )
    mixed = (base + adapter_out).astype(jnp.bfloat16)
    grad_b_local = jnp.dot(low_wide, output_gradient, preferred_element_type=jnp.float32).reshape(
        job_count, rank_count, local_width
    )
    grad_a_local = jnp.dot(back_wide, hidden, preferred_element_type=jnp.float32).reshape(
        job_count, rank_count, local_hidden
    )
    total_a, total_b = (
        lax.psum(grad_a_local.astype(jnp.bfloat16), "dp").astype(jnp.float32),
        lax.psum(grad_b_local.astype(jnp.bfloat16), "dp").astype(jnp.float32),
    )
    share = job_count // lax.axis_size("dp")
    offset = lax.axis_index("dp") * share
    grad_a = lax.dynamic_slice_in_dim(total_a, offset, share, 0)
    grad_b = lax.dynamic_slice_in_dim(total_b, offset, share, 0)
    weight_cols = down_matrix
    through = lax.dot_general(
        lax.all_gather(output_gradient, "tensor", axis=1, tiled=True),
        weight_cols,
        dims,
        preferred_element_type=jnp.float32,
    )
    adapter_back = lax.dot_general(
        back_wide, input_adapter, lead, preferred_element_type=jnp.float32
    )
    grad_hidden = (through + adapter_back).astype(jnp.bfloat16)
    return (mixed, grad_hidden, grad_a, grad_b)


Z, Y = 4, 2
MESH = pl.DeviceIdType.MESH
F32, BF16 = jnp.float32, jnp.bfloat16


def fused_kernel(
    job_ref, hidden_ref, in_ref, out_ref, og_ref, w_ref,
    mixed_ref, gh_ref, ga_ref, gb_ref,
    gat, part, wbuf, acc, adp, ray, raz, rbz, rby, xs, xr, lw, bw, gsend_a, gsend_b, grecv_a, grecv_b,
    wsem, azs, azr, ays, ayr, bys, byr, bzs, bzr,
    rays, rayr, razs, razr, rbzs, rbzr, rbys, rbyr, xss, xrs, gss, grs,
):
    rows, lh = hidden_ref.shape
    lwid = og_ref.shape[1]
    wide = in_ref.shape[0]
    ra, rb = ray.shape[1], rby.shape[0]
    sa, sb = pl.ds(0, ra), pl.ds(ra, rb)
    half = ga_ref.shape[0]
    dp = lax.axis_index("dp")
    t = lax.axis_index("tensor")
    z, y = t // Y, t % Y
    oy = 1 - y
    tl, tr, ty = jnp.maximum(t - Y, 0), jnp.minimum(t + Y, Z * Y - 1), z * Y + oy
    t1, t2 = (z + 1 - 2 * (z % 2)) * Y + y, ((z + 2) % Z) * Y + y
    hop = (tr, tl)

    def cp(a, b, ss, rs, dst):
        return pltpu.make_async_remote_copy(
            src_ref=a, dst_ref=b, send_sem=ss, recv_sem=rs,
            device_id={"tensor": dst}, device_id_type=MESH)

    def cpd(a, b, ss, rs):
        return pltpu.make_async_remote_copy(
            src_ref=a, dst_ref=b, send_sem=ss, recv_sem=rs,
            device_id={"dp": 1 - dp}, device_id_type=MESH)

    col = (y, oy)

    def ag_az(d, zs, own=False):
        s = zs * Y + y
        a = og_ref.at[sa] if own else gat.at[s, sa]
        return cp(a, gat.at[s, sa], azs.at[d, zs], azr.at[zs], hop[d])

    def ag_ay(zs, own=False):
        s = zs * Y + y
        a = og_ref.at[sa] if own else gat.at[s, sa]
        return cp(a, gat.at[s, sa], ays.at[zs], ayr.at[zs], ty)

    def ag_by():
        return cp(og_ref.at[sb], gat.at[t, sb], bys, byr, ty)

    def ag_bz(d, zs, rel, own=False):
        s = zs * Y + col[rel]
        a = og_ref.at[sb] if own else gat.at[s, sb]
        return cp(a, gat.at[s, sb], bzs.at[d, zs, rel], bzr.at[zs, rel], hop[d])

    def rs_ay(d):
        return cp(part.at[d * Y + oy, sa], ray.at[d], rays.at[d], rayr.at[d], ty)

    def rs_az(k, d):
        return cp(part.at[d * Y + y, sa], raz.at[k, d], razs.at[k, d], razr.at[k, d], hop[k])

    def rs_bz(k, d, rel):
        return cp(part.at[d * Y + col[rel], sb], rbz.at[k, d, rel], rbzs.at[k, d, rel],
                  rbzr.at[k, d, rel], hop[k])

    def rs_by():
        return cp(part.at[z * Y + oy, sb], rby, rbys, rbyr, ty)

    def exch(i):
        return cp(xs.at[i], xr.at[i], xss.at[i], xrs.at[i], (ty, t1, t2)[i])

    def block_of(s):
        q = (s % (Z * Y)) // Y
        r = s % Y
        low_z = z < Z // 2
        far = jnp.where(low_z, Z - 1 - q, q)
        zm = jnp.where(low_z, z, Z - 1 - z)
        near = jnp.where((zm == 1) & (q < 2), 1 - q, q)
        near = jnp.where(low_z, near, Z - 1 - near)
        first = s < Z * Y
        zz = jnp.where(first, far, near)
        return zz, jnp.where(first, jnp.where(r == 0, oy, y), jnp.where(r == 0, y, oy))

    slots = wbuf.shape[0]

    def wcopy(s):
        zz, yy = block_of(s)
        c = pl.multiple_of((zz * Y + yy) * lwid, lwid)
        return pltpu.make_async_copy(
            w_ref.at[:, pl.ds(c, lwid)], wbuf.at[s % slots], wsem.at[s % slots])

    steps = 2 * Z * Y

    barrier = pltpu.get_barrier_semaphore()

    def greet(**dev):
        pl.semaphore_signal(barrier, inc=1, device_id=dev, device_id_type=MESH)

    greet(tensor=ty)
    greet(tensor=t2)
    greet(dp=1 - dp)

    @pl.when(z > 0)
    def _():
        greet(tensor=tl)

    @pl.when(z < Z - 1)
    def _():
        greet(tensor=tr)

    wcopy(0).start()
    wcopy(1).start()
    inner = (z > 0) & (z < Z - 1)

    @pl.when(inner)
    def _():
        pl.semaphore_wait(barrier, 5)

    @pl.when(jnp.logical_not(inner))
    def _():
        pl.semaphore_wait(barrier, 4)

    has = (z < Z - 1, z > 0)
    from_side = (z > 0, z < Z - 1)
    ag_by().start()
    for k in range(2):
        @pl.when(has[k])
        def _(k=k):
            ag_az(k, z, True).start()
            ag_bz(k, z, 0, True).start()
    ag_ay(z, True).start()

    gat[t] = og_ref[...]

    tile = 128
    jobs = tile // 16
    job = job_ref[...]

    def mask_of(n):
        r = lax.broadcasted_iota(jnp.int32, (tile, rows), 0) + n * tile
        return (r // 16) == job

    nt = (((1,), (1,)), ((), ()))
    tn = (((0,), (0,)), ((), ()))

    def low_tile(a_ref, b_ref, n):
        v = lax.dot_general(a_ref[pl.ds(pl.multiple_of(n * tile, tile), tile), :], b_ref[...], nt,
                            preferred_element_type=F32)
        v = jnp.where(mask_of(n), v, 0.0)
        return jnp.sum(v.reshape(jobs, 16, rows), axis=0)

    zero = jnp.zeros((16, rows), F32)

    xs[0, pl.ds(0, 16)] = lax.fori_loop(
        0, wide // tile, lambda n, c: c + low_tile(in_ref, hidden_ref, n), zero)
    xs[0, pl.ds(16, 16)] = lax.fori_loop(
        0, wide // tile, lambda n, c: c + low_tile(out_ref, og_ref, n), zero)
    exch(0).start()

    nw = 256

    def next_w(s):
        wcopy(s).wait()

        @pl.when(s + 2 < steps)
        def _():
            wcopy(s + 2).start()

    def forward_step(s, c):
        next_w(s)
        zz, yy = block_of(s)
        slot = s % slots
        b = zz * Y + yy

        def inner_tile(n, c):
            cs = pl.ds(pl.multiple_of(n * nw, nw), nw)
            part[b, :, cs] = jnp.dot(
                hidden_ref[...], wbuf[slot, :, cs], preferred_element_type=F32).astype(BF16)
            return c

        lax.fori_loop(0, lwid // nw, inner_tile, 0)

        @pl.when(s % Y == 0)
        def _():
            rs_ay(zz).start()
        return c

    def back_step(s):
        next_w(s)
        zz, yy = block_of(s)
        slot = s % slots
        b = zz * Y + yy

        def inner_tile(n, c):
            cs = pl.ds(pl.multiple_of(n * nw, nw), nw)
            acc[:, cs] += lax.dot_general(
                gat[b], wbuf[slot, cs, :], nt, preferred_element_type=F32)
            return c

        lax.fori_loop(0, lh // nw, inner_tile, 0)

    step_rows = 48

    def add_into(dst, srcs, n):
        def go(i, c):
            rs = pl.ds(pl.multiple_of(i * step_rows, step_rows), step_rows)
            v = dst[rs, :].astype(F32)
            for x in srcs:
                v = v + x[rs, :].astype(F32)
            dst[rs, :] = v.astype(dst.dtype)
            return c
        lax.fori_loop(0, n // step_rows, go, 0)

    def ag_round(k):
        for d in range(2):
            zs = z - k if d == 0 else z + k
            ok = zs >= 0 if d == 0 else zs < Z
            zc = jnp.clip(zs, 0, Z - 1)

            @pl.when(ok)
            def _(d=d, zc=zc):
                ag_az(d, zc).wait_recv()

                @pl.when(has[d])
                def _():
                    ag_az(d, zc).start()
                ag_ay(zc).start()
        for rel in range(2):
            for d in range(2):
                zs = z - k if d == 0 else z + k
                ok = zs >= 0 if d == 0 else zs < Z
                zc = jnp.clip(zs, 0, Z - 1)

                @pl.when(ok)
                def _(d=d, zc=zc, rel=rel):
                    ag_bz(d, zc, rel).wait_recv()

                    @pl.when(has[d])
                    def _():
                        ag_bz(d, zc, rel).start()

    def rs_round(r):
        for k in range(2):
            pos = z if k == 0 else Z - 1 - z
            dd = Z - 1 - r + pos if k == 0 else r - pos
            d = jnp.clip(dd, 0, Z - 1)

            @pl.when(r >= pos)
            def _(k=k, d=d):
                for rel in (1, 0):
                    @pl.when(from_side[k])
                    def _(rel=rel):
                        rs_bz(k, d, rel).wait_recv()
                        add_into(part.at[d * Y + col[rel], sb], [rbz.at[k, d, rel]], rb)
                    rs_bz(k, d, rel).start()
                rs_ay(d).wait_recv()

                @pl.when(from_side[k])
                def _():
                    rs_az(k, d).wait_recv()
                    add_into(part.at[d * Y + y, sa], [ray.at[d], raz.at[k, d]], ra)

                @pl.when(jnp.logical_not(from_side[k]))
                def _():
                    add_into(part.at[d * Y + y, sa], [ray.at[d]], ra)
                rs_az(k, d).start()

    lax.fori_loop(0, Z, forward_step, 0)
    ag_by().wait_recv()
    for k in range(2):
        @pl.when(has[k])
        def _(k=k):
            ag_bz(k, z, 1).start()
    exch(0).wait_recv()
    xs[1] = xs[0] + xr[0]
    exch(1).start()
    lax.fori_loop(Z, 2 * Z, forward_step, 0)
    exch(1).wait_recv()
    xs[2] = xs[1] + xr[1]
    exch(2).start()
    rs_round(0)
    ag_round(1)
    exch(2).wait_recv()
    low = SCALE * (xs[2, pl.ds(0, 16)] + xr[2, pl.ds(0, 16)])
    back = SCALE * (xs[2, pl.ds(16, 16)] + xr[2, pl.ds(16, 16)])
    low8 = jnp.concatenate([low] * jobs, axis=0)
    back8 = jnp.concatenate([back] * jobs, axis=0)
    for n in range(wide // tile):
        m = mask_of(n)
        lw[pl.ds(n * tile, tile), :] = jnp.where(m, low8, 0.0).astype(BF16)
        bw[pl.ds(n * tile, tile), :] = jnp.where(m, back8, 0.0).astype(BF16)

    theirs = pl.ds(pl.multiple_of((1 - dp) * half, half), half)
    mine = pl.ds(pl.multiple_of(dp * half, half), half)
    gtile = 256

    def cols_loop(n, f):
        def go(i, c):
            f(pl.ds(pl.multiple_of(i * gtile, gtile), gtile))
            return c
        lax.fori_loop(0, n // gtile, go, 0)

    def send_a(cs):
        gsend_a[:, cs] = jnp.dot(bw[theirs, :], hidden_ref[:, cs], preferred_element_type=F32).astype(BF16)

    def send_b(cs):
        gsend_b[:, cs] = jnp.dot(lw[theirs, :], og_ref[:, cs], preferred_element_type=F32).astype(BF16)

    def init_acc(cs):
        acc[:, cs] = lax.dot_general(bw[...], in_ref[:, cs], tn, preferred_element_type=F32)

    def init_adp(cs):
        adp[:, cs] = lax.dot_general(lw[...], out_ref[:, cs], tn, preferred_element_type=F32)

    g_a = cpd(gsend_a, grecv_a, gss.at[0], grs.at[0])
    g_b = cpd(gsend_b, grecv_b, gss.at[1], grs.at[1])
    cols_loop(lh, send_a)
    g_a.start()
    cols_loop(lwid, send_b)
    g_b.start()
    cols_loop(lh, init_acc)

    def back_pair(q):
        s = Z * Y + q * Y
        back_step(s)
        zz, _ = block_of(s)
        ag_ay(zz).wait_recv()
        back_step(s + 1)

    back_pair(0)
    rs_round(1)
    ag_round(2)
    cols_loop(lwid, init_adp)

    g_a.wait_recv()
    g_b.wait_recv()

    def own_a(cs):
        ga_ref[:, cs] = jnp.dot(bw[mine, :], hidden_ref[:, cs], preferred_element_type=F32) + grecv_a[:, cs].astype(F32)

    def own_b(cs):
        gb_ref[:, cs] = jnp.dot(lw[mine, :], og_ref[:, cs], preferred_element_type=F32) + grecv_b[:, cs].astype(F32)

    cols_loop(lh, own_a)
    cols_loop(lwid, own_b)
    back_pair(1)
    rs_round(2)
    ag_round(3)
    back_pair(2)

    for k in range(2):
        @pl.when(from_side[k])
        def _(k=k):
            rs_bz(k, z, 1).wait_recv()
            add_into(part.at[z * Y + oy, sb], [rbz.at[k, z, 1]], rb)
    rs_by().start()
    rs_ay(z).wait_recv()
    add_into(adp.at[sa], [part.at[t, sa], ray.at[z]], ra)
    add_into(adp.at[sb], [part.at[t, sb]], rb)
    for k in range(2):
        @pl.when(from_side[k])
        def _(k=k):
            rs_bz(k, z, 0).wait_recv()
            add_into(adp.at[sb], [rbz.at[k, z, 0]], rb)
            rs_az(k, z).wait_recv()
            add_into(adp.at[sa], [raz.at[k, z]], ra)
    back_pair(3)

    def end_gh(cs):
        gh_ref[:, cs] = acc[:, cs].astype(BF16)

    cols_loop(lh, end_gh)
    rs_by().wait_recv()
    add_into(adp.at[sb], [rby], rb)

    def end_mixed(cs):
        mixed_ref[:, cs] = adp[:, cs].astype(BF16)

    cols_loop(lwid, end_mixed)

    g_a.wait_send()
    g_b.wait_send()
    ag_by().wait_send()
    rs_by().wait_send()
    for i in range(3):
        exch(i).wait_send()
    for d in range(Z):
        ag_ay(d).wait_send()
        rs_ay(d).wait_send()
        for k in range(2):
            @pl.when((d <= z if k == 0 else d >= z) & has[k])
            def _(k=k, d=d):
                ag_az(k, d).wait_send()
                ag_bz(k, d, 0).wait_send()
                ag_bz(k, d, 1).wait_send()

            @pl.when(d > z if k == 0 else d < z)
            def _(k=k, d=d):
                rs_az(k, d).wait_send()
                rs_bz(k, d, 0).wait_send()
                rs_bz(k, d, 1).wait_send()


def fused_body(hidden, down_matrix, rank_input_map, rank_output_map, job_row_counts, output_gradient):
    rows, lh = hidden.shape
    job_count, rank_count, lwid = rank_output_map.shape
    wide = job_count * rank_count
    positions = lax.axis_index("dp") * rows + lax.iota(jnp.int32, rows)
    ends = jnp.cumsum(job_row_counts)
    job = jnp.sum((ends[:, None] <= positions[None, :]).astype(jnp.int32), axis=0)[None, :]
    rb = (rows * 3 // 8) // 48 * 48
    ra = rows - rb
    n = Z * Y
    half = wide // 2
    dma = pltpu.SemaphoreType.DMA
    vm = pl.BlockSpec(memory_space=pltpu.VMEM)
    mixed, gh, ga, gb = pl.pallas_call(
        fused_kernel,
        out_shape=(
            jax.ShapeDtypeStruct((rows, lwid), BF16),
            jax.ShapeDtypeStruct((rows, lh), BF16),
            jax.ShapeDtypeStruct((half, lh), F32),
            jax.ShapeDtypeStruct((half, lwid), F32),
        ),
        in_specs=[vm, vm, vm, vm, vm, pl.BlockSpec(memory_space=pl.ANY)],
        out_specs=(vm, vm, vm, vm),
        scratch_shapes=[
            pltpu.VMEM((n, rows, lwid), BF16),
            pltpu.VMEM((n, rows, lwid), BF16),
            pltpu.VMEM((3, lh, lwid), BF16),
            pltpu.VMEM((rows, lh), F32),
            pltpu.VMEM((rows, lwid), F32),
            pltpu.VMEM((Z, ra, lwid), BF16),
            pltpu.VMEM((2, Z, ra, lwid), BF16),
            pltpu.VMEM((2, Z, 2, rb, lwid), BF16),
            pltpu.VMEM((rb, lwid), BF16),
            pltpu.VMEM((3, 2 * rank_count, rows), F32),
            pltpu.VMEM((3, 2 * rank_count, rows), F32),
            pltpu.VMEM((wide, rows), BF16),
            pltpu.VMEM((wide, rows), BF16),
            pltpu.VMEM((half, lh), BF16),
            pltpu.VMEM((half, lwid), BF16),
            pltpu.VMEM((half, lh), BF16),
            pltpu.VMEM((half, lwid), BF16),
            dma((3,)),
            dma((2, Z)), dma((Z,)), dma((Z,)), dma((Z,)), dma, dma, dma((2, Z, 2)), dma((Z, 2)),
            dma((Z,)), dma((Z,)), dma((2, Z)), dma((2, Z)), dma((2, Z, 2)), dma((2, Z, 2)), dma, dma,
            dma((3,)), dma((3,)), dma((2,)), dma((2,)),
        ],
        compiler_params=pltpu.CompilerParams(
            collective_id=0, has_side_effects=True, vmem_limit_bytes=62 * 1024 * 1024),
    )(
        job, hidden, rank_input_map.reshape(wide, lh), rank_output_map.reshape(wide, lwid),
        output_gradient, down_matrix,
    )
    share = job_count // 2
    return mixed, gh, ga.reshape(share, rank_count, lh), gb.reshape(share, rank_count, lwid)


def solution(mesh):
    placed = (
        P(("groups", "dp"), "tensor"),
        P("tensor", None),
        P(None, None, "tensor"),
        P(None, None, "tensor"),
        P("groups"),
        P(("groups", "dp"), "tensor"),
    )
    return jax.shard_map(
        fused_body if mesh.shape["tensor"] == Z * Y else body,
        mesh=mesh,
        in_specs=placed,
        out_specs=(
            P(("groups", "dp"), "tensor"),
            P(("groups", "dp"), "tensor"),
            P(("groups", "dp"), None, "tensor"),
            P(("groups", "dp"), None, "tensor"),
        ),
        check_vma=False,
    )
```

```python
import jax
import jax.numpy as jnp
from jax import lax
from jax.experimental import pallas as pl
from jax.experimental.pallas import tpu as pltpu
from jax.sharding import PartitionSpec as P

SCALE = 2.0


def select(spread, member, rank_count):
    job_count = member.shape[0]
    return jnp.sum(
        spread.reshape(job_count, rank_count, member.shape[1]) * member[:, None, :], axis=0
    )


def expand(values, member):
    job_count, rows = member.shape
    full = member[:, None, :] * values.astype(jnp.float32)[None, :, :]
    return full.reshape(job_count * values.shape[0], rows).astype(jnp.bfloat16)


def body(hidden, down_matrix, rank_input_map, rank_output_map, job_row_counts, output_gradient):
    rows_dev, local_hidden = hidden.shape
    job_count, rank_count, local_width = rank_output_map.shape
    input_adapter = rank_input_map.reshape(job_count * rank_count, local_hidden)
    output_adapter = rank_output_map.reshape(job_count * rank_count, local_width)
    positions = lax.axis_index("dp") * rows_dev + lax.iota(jnp.int32, rows_dev)
    ends = jnp.cumsum(job_row_counts)
    starts = ends - job_row_counts
    member = (
        (positions[None, :] >= starts[:, None]) & (positions[None, :] < ends[:, None])
    ).astype(jnp.float32)
    dims = (((1,), (1,)), ((), ()))
    lead = (((0,), (0,)), ((), ()))
    low_part = select(
        lax.dot_general(input_adapter, hidden, dims, preferred_element_type=jnp.float32),
        member,
        rank_count,
    )
    back_part = select(
        lax.dot_general(output_adapter, output_gradient, dims, preferred_element_type=jnp.float32),
        member,
        rank_count,
    )
    low = lax.psum(low_part, "tensor")
    back_low = lax.psum(back_part, "tensor")
    low_wide = expand((SCALE * low).astype(jnp.bfloat16), member)
    back_wide = expand((SCALE * back_low).astype(jnp.bfloat16), member)
    cross = (((0,), (1,)), ((), ()))
    weight_cols = down_matrix
    base = (
        lax.psum_scatter(
            lax.dot_general(weight_cols, hidden, cross, preferred_element_type=jnp.float32).astype(
                jnp.bfloat16
            ),
            "tensor",
            scatter_dimension=0,
            tiled=True,
        )
        .astype(jnp.float32)
        .T
    )
    adapter_out = lax.dot_general(
        low_wide, output_adapter, lead, preferred_element_type=jnp.float32
    )
    mixed = (base + adapter_out).astype(jnp.bfloat16)
    grad_b_local = jnp.dot(low_wide, output_gradient, preferred_element_type=jnp.float32).reshape(
        job_count, rank_count, local_width
    )
    grad_a_local = jnp.dot(back_wide, hidden, preferred_element_type=jnp.float32).reshape(
        job_count, rank_count, local_hidden
    )
    total_a, total_b = (
        lax.psum(grad_a_local.astype(jnp.bfloat16), "dp").astype(jnp.float32),
        lax.psum(grad_b_local.astype(jnp.bfloat16), "dp").astype(jnp.float32),
    )
    share = job_count // lax.axis_size("dp")
    offset = lax.axis_index("dp") * share
    grad_a = lax.dynamic_slice_in_dim(total_a, offset, share, 0)
    grad_b = lax.dynamic_slice_in_dim(total_b, offset, share, 0)
    weight_cols = down_matrix
    through = lax.dot_general(
        lax.all_gather(output_gradient, "tensor", axis=1, tiled=True),
        weight_cols,
        dims,
        preferred_element_type=jnp.float32,
    )
    adapter_back = lax.dot_general(
        back_wide, input_adapter, lead, preferred_element_type=jnp.float32
    )
    grad_hidden = (through + adapter_back).astype(jnp.bfloat16)
    return (mixed, grad_hidden, grad_a, grad_b)


Z, Y = 4, 2
CHUNKS = 2
MESH = pl.DeviceIdType.MESH
F32, BF16 = jnp.float32, jnp.bfloat16


def fused_kernel(
    job_ref, hidden_ref, in_ref, out_ref, og_ref, w_ref,
    mixed_ref, gh_ref, ga_ref, gb_ref,
    gat, part, wbuf, acc, adp, ray, raz, rbz, rby, xs, xr, lw, bw, gsend_a, gsend_b, grecv_a, grecv_b,
    wsem, azs, azr, ays, ayr, bys, byr, bzs, bzr,
    rays, rayr, razs, razr, rbzs, rbzr, rbys, rbyr, xss, xrs, gss, grs,
):
    rows, lh = hidden_ref.shape
    lwid = og_ref.shape[1]
    wide = in_ref.shape[0]
    ra, rb = ray.shape[1], rby.shape[0]
    rac, rbc = ra // CHUNKS, rb // CHUNKS
    sa = [pl.ds(c * rac, rac) for c in range(CHUNKS)]
    sb = [pl.ds(ra + c * rbc, rbc) for c in range(CHUNKS)]
    sb0 = [pl.ds(c * rbc, rbc) for c in range(CHUNKS)]
    half = ga_ref.shape[0]
    dp = lax.axis_index("dp")
    t = lax.axis_index("tensor")
    z, y = t // Y, t % Y
    oy = 1 - y
    tl, tr, ty = jnp.maximum(t - Y, 0), jnp.minimum(t + Y, Z * Y - 1), z * Y + oy
    t1, t2 = (z + 1 - 2 * (z % 2)) * Y + y, ((z + 2) % Z) * Y + y
    hop = (tr, tl)

    def cp(a, b, ss, rs, dst):
        return pltpu.make_async_remote_copy(
            src_ref=a, dst_ref=b, send_sem=ss, recv_sem=rs,
            device_id={"tensor": dst}, device_id_type=MESH)

    def cpd(a, b, ss, rs):
        return pltpu.make_async_remote_copy(
            src_ref=a, dst_ref=b, send_sem=ss, recv_sem=rs,
            device_id={"dp": 1 - dp}, device_id_type=MESH)

    col = (y, oy)

    def ag_az(c, d, zs, own=False):
        s = zs * Y + y
        a = og_ref.at[sa[c]] if own else gat.at[s, sa[c]]
        return cp(a, gat.at[s, sa[c]], azs.at[d, zs, c], azr.at[zs, c], hop[d])

    def ag_ay(c, zs, own=False):
        s = zs * Y + y
        a = og_ref.at[sa[c]] if own else gat.at[s, sa[c]]
        return cp(a, gat.at[s, sa[c]], ays.at[zs, c], ayr.at[zs, c], ty)

    def ag_by(c):
        return cp(og_ref.at[sb[c]], gat.at[t, sb[c]], bys.at[c], byr.at[c], ty)

    def ag_bz(c, d, zs, rel, own=False):
        s = zs * Y + col[rel]
        a = og_ref.at[sb[c]] if own else gat.at[s, sb[c]]
        return cp(a, gat.at[s, sb[c]], bzs.at[d, zs, rel, c], bzr.at[zs, rel, c], hop[d])

    def rs_ay(c, d):
        return cp(part.at[d * Y + oy, sa[c]], ray.at[d, sa[c]], rays.at[d, c], rayr.at[d, c], ty)

    def rs_az(c, k, d):
        return cp(part.at[d * Y + y, sa[c]], raz.at[k, d, sa[c]], razs.at[k, d, c],
                  razr.at[k, d, c], hop[k])

    def rs_bz(c, k, d, rel):
        return cp(part.at[d * Y + col[rel], sb[c]], rbz.at[k, d, rel, sb0[c]], rbzs.at[k, d, rel, c],
                  rbzr.at[k, d, rel, c], hop[k])

    def rs_by(c):
        return cp(part.at[z * Y + oy, sb[c]], rby.at[sb0[c]], rbys.at[c], rbyr.at[c], ty)

    def exch(i):
        return cp(xs.at[i], xr.at[i], xss.at[i], xrs.at[i], (ty, t1, t2)[i])

    def block_of(s):
        q = (s % (Z * Y)) // Y
        r = s % Y
        low_z = z < Z // 2
        far = jnp.where(low_z, Z - 1 - q, q)
        zm = jnp.where(low_z, z, Z - 1 - z)
        near = jnp.where((zm == 1) & (q < 2), 1 - q, q)
        near = jnp.where(low_z, near, Z - 1 - near)
        first = s < Z * Y
        zz = jnp.where(first, far, near)
        return zz, jnp.where(first, jnp.where(r == 0, oy, y), jnp.where(r == 0, y, oy))

    slots = wbuf.shape[0]

    def wcopy(s):
        zz, yy = block_of(s)
        c = pl.multiple_of((zz * Y + yy) * lwid, lwid)
        return pltpu.make_async_copy(
            w_ref.at[:, pl.ds(c, lwid)], wbuf.at[s % slots], wsem.at[s % slots])

    steps = 2 * Z * Y

    barrier = pltpu.get_barrier_semaphore()

    def greet(**dev):
        pl.semaphore_signal(barrier, inc=1, device_id=dev, device_id_type=MESH)

    greet(tensor=ty)
    greet(tensor=t2)
    greet(dp=1 - dp)

    @pl.when(z > 0)
    def _():
        greet(tensor=tl)

    @pl.when(z < Z - 1)
    def _():
        greet(tensor=tr)

    wcopy(0).start()
    wcopy(1).start()
    inner = (z > 0) & (z < Z - 1)

    @pl.when(inner)
    def _():
        pl.semaphore_wait(barrier, 5)

    @pl.when(jnp.logical_not(inner))
    def _():
        pl.semaphore_wait(barrier, 4)

    has = (z < Z - 1, z > 0)
    from_side = (z > 0, z < Z - 1)
    for c in range(CHUNKS):
        ag_by(c).start()
    for c in range(CHUNKS):
        for k in range(2):
            @pl.when(has[k])
            def _(k=k, c=c):
                ag_az(c, k, z, True).start()
                ag_bz(c, k, z, 0, True).start()
        ag_ay(c, z, True).start()

    gat[t] = og_ref[...]

    tile = 128
    jobs = tile // 16
    job = job_ref[...]

    def mask_of(n):
        r = lax.broadcasted_iota(jnp.int32, (tile, rows), 0) + n * tile
        return (r // 16) == job

    nt = (((1,), (1,)), ((), ()))
    tn = (((0,), (0,)), ((), ()))

    def low_tile(a_ref, b_ref, n):
        v = lax.dot_general(a_ref[pl.ds(pl.multiple_of(n * tile, tile), tile), :], b_ref[...], nt,
                            preferred_element_type=F32)
        v = jnp.where(mask_of(n), v, 0.0)
        return jnp.sum(v.reshape(jobs, 16, rows), axis=0)

    zero = jnp.zeros((16, rows), F32)

    xs[0, pl.ds(0, 16)] = lax.fori_loop(
        0, wide // tile, lambda n, c: c + low_tile(in_ref, hidden_ref, n), zero)
    xs[0, pl.ds(16, 16)] = lax.fori_loop(
        0, wide // tile, lambda n, c: c + low_tile(out_ref, og_ref, n), zero)
    exch(0).start()

    nw = 256

    def next_w(s):
        wcopy(s).wait()

        @pl.when(s + 2 < steps)
        def _():
            wcopy(s + 2).start()

    def forward_step(s, c):
        next_w(s)
        zz, yy = block_of(s)
        slot = s % slots
        b = zz * Y + yy

        def inner_tile(n, c):
            cs = pl.ds(pl.multiple_of(n * nw, nw), nw)
            part[b, :, cs] = jnp.dot(
                hidden_ref[...], wbuf[slot, :, cs], preferred_element_type=F32).astype(BF16)
            return c

        lax.fori_loop(0, lwid // nw, inner_tile, 0)

        @pl.when(s % Y == 0)
        def _():
            for p in range(CHUNKS):
                rs_ay(p, zz).start()
        return c

    def back_step(s, last=False):
        next_w(s)
        zz, yy = block_of(s)
        slot = s % slots
        b = zz * Y + yy

        def inner_tile(n, c):
            cs = pl.ds(pl.multiple_of(n * nw, nw), nw)
            v = acc[:, cs] + lax.dot_general(
                gat[b], wbuf[slot, cs, :], nt, preferred_element_type=F32)
            if last:
                gh_ref[:, cs] = v.astype(BF16)
            else:
                acc[:, cs] = v
            return c

        lax.fori_loop(0, lh // nw, inner_tile, 0)

    step_rows = 16

    def add_into(dst, srcs, n):
        def go(i, c):
            rs = pl.ds(pl.multiple_of(i * step_rows, step_rows), step_rows)
            v = dst[rs, :].astype(F32)
            for x in srcs:
                v = v + x[rs, :].astype(F32)
            dst[rs, :] = v.astype(dst.dtype)
            return c
        lax.fori_loop(0, n // step_rows, go, 0)

    def ag_round(k):
        for c in range(CHUNKS):
            for d in range(2):
                zs = z - k if d == 0 else z + k
                ok = zs >= 0 if d == 0 else zs < Z
                zc = jnp.clip(zs, 0, Z - 1)

                @pl.when(ok)
                def _(d=d, zc=zc, c=c):
                    ag_az(c, d, zc).wait_recv()

                    @pl.when(has[d])
                    def _():
                        ag_az(c, d, zc).start()
                    ag_ay(c, zc).start()
            for rel in range(2):
                for d in range(2):
                    zs = z - k if d == 0 else z + k
                    ok = zs >= 0 if d == 0 else zs < Z
                    zc = jnp.clip(zs, 0, Z - 1)

                    @pl.when(ok)
                    def _(d=d, zc=zc, rel=rel, c=c):
                        ag_bz(c, d, zc, rel).wait_recv()

                        @pl.when(has[d])
                        def _():
                            ag_bz(c, d, zc, rel).start()

    def rs_round(r):
        for c in range(CHUNKS):
            for k in range(2):
                pos = z if k == 0 else Z - 1 - z
                dd = Z - 1 - r + pos if k == 0 else r - pos
                d = jnp.clip(dd, 0, Z - 1)

                @pl.when(r >= pos)
                def _(k=k, d=d, c=c):
                    for rel in (1, 0):
                        @pl.when(from_side[k])
                        def _(rel=rel):
                            rs_bz(c, k, d, rel).wait_recv()
                            add_into(part.at[d * Y + col[rel], sb[c]], [rbz.at[k, d, rel, sb0[c]]], rbc)
                        rs_bz(c, k, d, rel).start()
                    rs_ay(c, d).wait_recv()

                    @pl.when(from_side[k])
                    def _():
                        rs_az(c, k, d).wait_recv()
                        add_into(part.at[d * Y + y, sa[c]], [ray.at[d, sa[c]], raz.at[k, d, sa[c]]], rac)

                    @pl.when(jnp.logical_not(from_side[k]))
                    def _():
                        add_into(part.at[d * Y + y, sa[c]], [ray.at[d, sa[c]]], rac)
                    rs_az(c, k, d).start()

    lax.fori_loop(0, Z, forward_step, 0)
    for c in range(CHUNKS):
        ag_by(c).wait_recv()
        for k in range(2):
            @pl.when(has[k])
            def _(k=k, c=c):
                ag_bz(c, k, z, 1).start()
    exch(0).wait_recv()
    xs[1] = xs[0] + xr[0]
    exch(1).start()
    lax.fori_loop(Z, 2 * Z, forward_step, 0)
    exch(1).wait_recv()
    xs[2] = xs[1] + xr[1]
    exch(2).start()
    rs_round(0)
    ag_round(1)
    exch(2).wait_recv()
    low = SCALE * (xs[2, pl.ds(0, 16)] + xr[2, pl.ds(0, 16)])
    back = SCALE * (xs[2, pl.ds(16, 16)] + xr[2, pl.ds(16, 16)])
    low8 = jnp.concatenate([low] * jobs, axis=0)
    back8 = jnp.concatenate([back] * jobs, axis=0)
    for n in range(wide // tile):
        m = mask_of(n)
        lw[pl.ds(n * tile, tile), :] = jnp.where(m, low8, 0.0).astype(BF16)
        bw[pl.ds(n * tile, tile), :] = jnp.where(m, back8, 0.0).astype(BF16)

    theirs = pl.ds(pl.multiple_of((1 - dp) * half, half), half)
    mine = pl.ds(pl.multiple_of(dp * half, half), half)
    gtile = 256

    def cols_loop(n, f):
        def go(i, c):
            f(pl.ds(pl.multiple_of(i * gtile, gtile), gtile))
            return c
        lax.fori_loop(0, n // gtile, go, 0)

    def send_a(cs):
        gsend_a[:, cs] = jnp.dot(bw[theirs, :], hidden_ref[:, cs], preferred_element_type=F32).astype(BF16)

    def send_b(cs):
        gsend_b[:, cs] = jnp.dot(lw[theirs, :], og_ref[:, cs], preferred_element_type=F32).astype(BF16)

    def init_acc(cs):
        acc[:, cs] = lax.dot_general(bw[...], in_ref[:, cs], tn, preferred_element_type=F32)

    def init_adp(cs):
        adp[:, cs] = lax.dot_general(lw[...], out_ref[:, cs], tn, preferred_element_type=F32)

    g_a = cpd(gsend_a, grecv_a, gss.at[0], grs.at[0])
    g_b = cpd(gsend_b, grecv_b, gss.at[1], grs.at[1])
    cols_loop(lh, send_a)
    g_a.start()
    cols_loop(lwid, send_b)
    g_b.start()
    cols_loop(lh, init_acc)

    def back_pair(q):
        s = Z * Y + q * Y
        back_step(s)
        zz, _ = block_of(s)
        for c in range(CHUNKS):
            ag_ay(c, zz).wait_recv()
        back_step(s + 1, q == Z - 1)

    back_pair(0)
    rs_round(1)
    ag_round(2)
    cols_loop(lwid, init_adp)

    g_a.wait_recv()
    g_b.wait_recv()

    def own_a(cs):
        ga_ref[:, cs] = jnp.dot(bw[mine, :], hidden_ref[:, cs], preferred_element_type=F32) + grecv_a[:, cs].astype(F32)

    def own_b(cs):
        gb_ref[:, cs] = jnp.dot(lw[mine, :], og_ref[:, cs], preferred_element_type=F32) + grecv_b[:, cs].astype(F32)

    cols_loop(lh, own_a)
    cols_loop(lwid, own_b)
    back_pair(1)
    rs_round(2)
    ag_round(3)
    back_pair(2)

    for c in range(CHUNKS):
        for k in range(2):
            @pl.when(from_side[k])
            def _(k=k, c=c):
                rs_bz(c, k, z, 1).wait_recv()
                add_into(part.at[z * Y + oy, sb[c]], [rbz.at[k, z, 1, sb0[c]]], rbc)
        rs_by(c).start()
        rs_ay(c, z).wait_recv()
        add_into(adp.at[sa[c]], [part.at[t, sa[c]], ray.at[z, sa[c]]], rac)
        add_into(adp.at[sb[c]], [part.at[t, sb[c]]], rbc)
        for k in range(2):
            @pl.when(from_side[k])
            def _(k=k, c=c):
                rs_bz(c, k, z, 0).wait_recv()
                add_into(adp.at[sb[c]], [rbz.at[k, z, 0, sb0[c]]], rbc)
                rs_az(c, k, z).wait_recv()
                add_into(adp.at[sa[c]], [raz.at[k, z, sa[c]]], rac)
    back_pair(3)

    for c in range(CHUNKS):
        rs_by(c).wait_recv()
        add_into(adp.at[sb[c]], [rby.at[sb0[c]]], rbc)

    def end_mixed(cs):
        mixed_ref[:, cs] = adp[:, cs].astype(BF16)

    cols_loop(lwid, end_mixed)

    g_a.wait_send()
    g_b.wait_send()
    for i in range(3):
        exch(i).wait_send()
    for c in range(CHUNKS):
        ag_by(c).wait_send()
        rs_by(c).wait_send()
        for d in range(Z):
            ag_ay(c, d).wait_send()
            rs_ay(c, d).wait_send()
            for k in range(2):
                @pl.when((d <= z if k == 0 else d >= z) & has[k])
                def _(k=k, d=d, c=c):
                    ag_az(c, k, d).wait_send()
                    ag_bz(c, k, d, 0).wait_send()
                    ag_bz(c, k, d, 1).wait_send()

                @pl.when(d > z if k == 0 else d < z)
                def _(k=k, d=d, c=c):
                    rs_az(c, k, d).wait_send()
                    rs_bz(c, k, d, 0).wait_send()
                    rs_bz(c, k, d, 1).wait_send()


def fused_body(hidden, down_matrix, rank_input_map, rank_output_map, job_row_counts, output_gradient):
    rows, lh = hidden.shape
    job_count, rank_count, lwid = rank_output_map.shape
    wide = job_count * rank_count
    positions = lax.axis_index("dp") * rows + lax.iota(jnp.int32, rows)
    ends = jnp.cumsum(job_row_counts)
    job = jnp.sum((ends[:, None] <= positions[None, :]).astype(jnp.int32), axis=0)[None, :]
    rb = (rows * 5 // 12) // (16 * CHUNKS) * (16 * CHUNKS)
    ra = rows - rb
    n = Z * Y
    half = wide // 2
    dma, cs = pltpu.SemaphoreType.DMA, CHUNKS
    vm = pl.BlockSpec(memory_space=pltpu.VMEM)
    mixed, gh, ga, gb = pl.pallas_call(
        fused_kernel,
        out_shape=(
            jax.ShapeDtypeStruct((rows, lwid), BF16),
            jax.ShapeDtypeStruct((rows, lh), BF16),
            jax.ShapeDtypeStruct((half, lh), F32),
            jax.ShapeDtypeStruct((half, lwid), F32),
        ),
        in_specs=[vm, vm, vm, vm, vm, pl.BlockSpec(memory_space=pl.ANY)],
        out_specs=(vm, vm, vm, vm),
        scratch_shapes=[
            pltpu.VMEM((n, rows, lwid), BF16),
            pltpu.VMEM((n, rows, lwid), BF16),
            pltpu.VMEM((3, lh, lwid), BF16),
            pltpu.VMEM((rows, lh), F32),
            pltpu.VMEM((rows, lwid), F32),
            pltpu.VMEM((Z, ra, lwid), BF16),
            pltpu.VMEM((2, Z, ra, lwid), BF16),
            pltpu.VMEM((2, Z, 2, rb, lwid), BF16),
            pltpu.VMEM((rb, lwid), BF16),
            pltpu.VMEM((3, 2 * rank_count, rows), F32),
            pltpu.VMEM((3, 2 * rank_count, rows), F32),
            pltpu.VMEM((wide, rows), BF16),
            pltpu.VMEM((wide, rows), BF16),
            pltpu.VMEM((half, lh), BF16),
            pltpu.VMEM((half, lwid), BF16),
            pltpu.VMEM((half, lh), BF16),
            pltpu.VMEM((half, lwid), BF16),
            dma((3,)),
            dma((2, Z, cs)), dma((Z, cs)), dma((Z, cs)), dma((Z, cs)), dma((cs,)), dma((cs,)),
            dma((2, Z, 2, cs)), dma((Z, 2, cs)),
            dma((Z, cs)), dma((Z, cs)), dma((2, Z, cs)), dma((2, Z, cs)),
            dma((2, Z, 2, cs)), dma((2, Z, 2, cs)), dma((cs,)), dma((cs,)),
            dma((3,)), dma((3,)), dma((2,)), dma((2,)),
        ],
        compiler_params=pltpu.CompilerParams(
            collective_id=0, has_side_effects=True, vmem_limit_bytes=62 * 1024 * 1024),
    )(
        job, hidden, rank_input_map.reshape(wide, lh), rank_output_map.reshape(wide, lwid),
        output_gradient, down_matrix,
    )
    share = job_count // 2
    return mixed, gh, ga.reshape(share, rank_count, lh), gb.reshape(share, rank_count, lwid)


def solution(mesh):
    placed = (
        P(("groups", "dp"), "tensor"),
        P("tensor", None),
        P(None, None, "tensor"),
        P(None, None, "tensor"),
        P("groups"),
        P(("groups", "dp"), "tensor"),
    )
    return jax.shard_map(
        fused_body if mesh.shape["tensor"] == Z * Y else body,
        mesh=mesh,
        in_specs=placed,
        out_specs=(
            P(("groups", "dp"), "tensor"),
            P(("groups", "dp"), "tensor"),
            P(("groups", "dp"), None, "tensor"),
            P(("groups", "dp"), None, "tensor"),
        ),
        check_vma=False,
    )
```
